32 devices in a mesh: dp: 8 (over z, x), mp: 4 (over y, core).
Axes of the slice: x: 2, y: 2, z: 4, core: 2. Of those that a mesh axis runs over, the one named last changes fastest.
Arguments:
- activations: bfloat16 [8192, 8192], P('dp', 'mp'), may hold values from -6 to 6
- out_grads: bfloat16 [8192, 14336], P('dp', 'mp'), may hold values from -0.29882812 to 0.29882812
- basis: bfloat16 [8192, 512], P('dp'), may hold values from -0.25 to 0.25
- first_moment: float32 [512, 14336], P('dp', 'mp'), may hold values from -3 to 3
- second_moment: float32 [512, 14336], P('dp', 'mp'), may hold values from 0.01 to 1
Outputs:
- update: bfloat16 [8192, 14336], P('dp', 'mp')
- moment_one: float32 [512, 14336], P('dp', 'mp')
- moment_two: float32 [512, 14336], P('dp', 'mp')
The draws below stay inside these ranges and needn't reach their ends.
All inputs are finite; a program needn't handle non-finite values.
Results may differ from the reference program's by a relative error of at most 0.0063.
Values may be sent and summed in bfloat16 or wider, within the bound.
No kernel may reach another device: no remote copies, remote signals or barrier semaphores. Data moves between devices by JAX's collectives and lax.ppermute only.
A program may use at most 128 MiB of HBM per device.

```python
import math
import jax
import jax.numpy as jnp
from jax import lax

D = 8192
FF = 14336
R = 512
STEP = 10
TOKENS = 8192


def shard_levels(key, dims, pieces, low, top_value):
    def one(dim, shards_of):
        steps = jax.random.uniform(jax.random.fold_in(jax.random.fold_in(key, 6), dim), (shards_of,), jnp.float32, low / len(pieces), top_value / len(pieces))
        return jnp.repeat(jnp.exp(steps), dims[dim] // shards_of).reshape((-1,) + (1,) * (len(dims) - dim - 1))

    factor_of = one(*pieces[0])
    for cut in pieces[1:]:
        factor_of = factor_of * one(*cut)
    return factor_of


def normal_values(key, extent, scale, reach, cuts=(), kind=jnp.bfloat16):
    gain = shard_levels(key, extent, cuts, -0.22, 0.18) if cuts else 1.0
    entries = jax.random.normal(key, extent, jnp.float32) * scale * gain
    return jnp.minimum(jnp.maximum(entries, -reach), reach).astype(kind)


def setup_inputs(seed: int = 0) -> dict:
    seeds = jax.random.split(jax.random.key(seed), 6)
    return {
        "activations": normal_values(seeds[0], (TOKENS, D), 1.0, 6.0, ((0, 8), (1, 4))),
        "out_grads": normal_values(seeds[1], (TOKENS, FF), 0.05, 0.29882812, ((0, 8), (1, 4))),
        "basis": normal_values(seeds[2], (D, R), R ** -0.5, 0.25, ((0, 8),)),
        "first_moment": normal_values(seeds[3], (R, FF), 0.5, 3.0, ((0, 8), (1, 4)), jnp.float32),
        "second_moment": jnp.clip(jnp.exp(math.log(1.0) - 4.6051702 * jax.random.uniform(seeds[4], (R, FF), jnp.float32) ** shard_levels(seeds[4], (R, FF), ((0, 8), (1, 4)), -0.2, 0.2)), 0.01, 1.0),
    }


BETA_ONE = 0.9
BETA_TWO = 0.999
ADAM_EPS = 1e-08

def reference(activations, out_grads, basis, first_moment, second_moment):
    projected = jnp.dot(activations, basis, preferred_element_type=jnp.float32).astype(jnp.bfloat16)
    gradient = lax.dot_general(projected, out_grads, (((0,), (0,)), ((), ())), preferred_element_type=jnp.float32)
    moment_one = BETA_ONE * first_moment + (1.0 - BETA_ONE) * gradient
    moment_two = BETA_TWO * second_moment + (1.0 - BETA_TWO) * gradient * gradient
    unbiased_one = moment_one / (1.0 - BETA_ONE ** STEP)
    unbiased_two = moment_two / (1.0 - BETA_TWO ** STEP)
    direction = (unbiased_one / (jnp.sqrt(unbiased_two) + ADAM_EPS)).astype(jnp.bfloat16)
    update = jnp.dot(basis, direction, preferred_element_type=jnp.float32).astype(jnp.bfloat16)
    return (update, moment_one, moment_two)
```

```python
import functools

import jax
import jax.numpy as jnp
from jax import lax
from jax.experimental import pallas as pl
from jax.experimental.pallas import tpu as pltpu
from jax.sharding import PartitionSpec as P

STEP = 10

BETA_ONE = 0.9
BETA_TWO = 0.999
ADAM_EPS = 1e-08

BF16 = jnp.bfloat16
F32 = jnp.float32
VMEM_LIMIT = 48 * 1024 * 1024
AXES = ("dp", "mp")


def tile_of(columns):
    for tile in (512, 256, 128):
        if columns % tile == 0:
            return tile
    return columns


def slot(line, r, n):
    rest = jnp.where(2 * line < n, 2 * line + r - n + 1, r)
    return jnp.where(line >= r, line - r, jnp.where(line + r < n, line + r, rest))


class Ring:
    def __init__(self, dp, mp):
        self.dp, self.mp, self.n = dp, mp, dp // 2

    def pairs(self, move):
        out = []
        for line in range(self.n):
            for pair in range(2):
                to = move(line, pair)
                if to is not None:
                    for m in range(self.mp):
                        out.append(((line * 2 + pair) * self.mp + m, (to[0] * 2 + to[1]) * self.mp + m))
        return out

    def swap(self, value):
        return lax.ppermute(value, AXES, self.pairs(lambda z, x: (z, 1 - x)))

    def up(self, value, valid):
        return lax.ppermute(value, AXES, self.pairs(lambda z, x: (z + 1, x) if z + 1 < self.n and valid(z) else None))

    def down(self, value, valid):
        return lax.ppermute(value, AXES, self.pairs(lambda z, x: (z - 1, x) if z > 0 and valid(z) else None))

    def gather(self, own):
        n = self.n
        line = lax.axis_index("dp") // 2
        ups, downs, others = [own], [own], [self.swap(own)]
        for r in range(1, n):
            ups.append(self.up(ups[-1], lambda z: z >= r - 1))
            downs.append(self.down(downs[-1], lambda z: z + r - 1 < n))
            value = jnp.where(line >= r, ups[r], downs[r])
            for k in range(1, r):
                users = [z for z in range(n) if z < r and z + r >= n and (2 * z + r - n + 1 if 2 * z < n else r) - z == k]
                for z in users:
                    value = jnp.where(line == z, downs[k], value)
            others.append(self.swap(value))
        return [own] + ups[1:] + downs[1:] + others

    def assemble(self, index_ref, blocks, out_ref):
        n = self.n
        rows = out_ref.shape[0] // self.dp
        line, pair = index_ref[0], index_ref[1]

        def put(ref, place, side):
            start = pl.multiple_of((place * 2 + side) * rows, rows)
            out_ref[pl.ds(start, rows), :] = ref[...]

        put(blocks[0], line, pair)
        for r in range(1, n):

            @pl.when(line >= r)
            def _(r=r):
                put(blocks[r], line - r, pair)

            @pl.when(line + r < n)
            def _(r=r):
                put(blocks[n - 1 + r], line + r, pair)

        for r in range(n):
            put(blocks[2 * n - 1 + r], slot(line, r, n), 1 - pair)

    def scatter_sum(self, send, keep):
        n = self.n
        line = lax.axis_index("dp") // 2
        got = [None] * n
        for r in reversed(range(n)):
            got[r] = self.swap(send[r])
        term = [keep[r].astype(F32) + got[r].astype(F32) for r in range(n)]
        from_above = from_below = None
        for k in reversed(range(1, n)):
            down = term[k]
            source = {}
            for z in range(n - k):
                r = k if z < k else (n - 1 - z + k if 2 * z < n else z + k)
                source.setdefault(r, []).append(z)
            up = None
            for r, places in source.items():
                if up is None:
                    up = term[r]
                else:
                    here = functools.reduce(jnp.logical_or, [line == z for z in places])
                    up = jnp.where(here, term[r], up)
            if from_above is not None:
                down = down + from_above.astype(F32)
                up = up + from_below.astype(F32)
            from_above = self.down(down.astype(BF16), lambda z: z >= k)
            from_below = self.up(up.astype(BF16), lambda z: z + k < n)
        return term[0] + from_above.astype(F32) + from_below.astype(F32)


def scatter_basis(basis, features, dp, mp):
    rows = basis.shape[0]
    piece = features // dp
    pairs = []
    for d in range(dp):
        for m in range(mp):
            start = m * features + d * piece
            pairs.append(((start // rows) * mp + (start % rows) // piece, d * mp + m))
    own = lax.dynamic_slice_in_dim(basis, lax.axis_index("mp") * piece, piece, 0)
    return lax.ppermute(own, AXES, pairs)


def project(ring, index, blocks, activations):
    tokens, features = activations.shape
    ranks = blocks[0].shape[1]
    mp = ring.mp
    half, step = mp // 2, tokens // mp

    def block_of(i, index):
        core, other = index[2], index[3]
        return jnp.where(i < half, 1 - core, core) * half + lax.rem(other + 1 + lax.rem(i, half), half)

    def kernel(index_ref, *refs):
        pieces, (act_ref, send_ref, keep_ref, held) = refs[: len(blocks)], refs[len(blocks) :]
        i = pl.program_id(0)

        @pl.when(i == 0)
        def _():
            ring.assemble(index_ref, pieces, held)

        value = jnp.dot(act_ref[...], held[...], preferred_element_type=F32)

        @pl.when(i < half)
        def _():
            send_ref[...] = value

        @pl.when(i >= half)
        def _():
            keep_ref[...] = value

    shape = jax.ShapeDtypeStruct((tokens // 2, ranks), F32)
    return pl.pallas_call(
        kernel,
        grid_spec=pltpu.PrefetchScalarGridSpec(
            num_scalar_prefetch=1,
            grid=(mp,),
            in_specs=[pl.BlockSpec(b.shape, lambda i, index: (0, 0)) for b in blocks]
            + [pl.BlockSpec((step, features), lambda i, index: (block_of(i, index), 0))],
            out_specs=[
                pl.BlockSpec((step, ranks), lambda i, index: (jnp.minimum(i, half - 1), 0)),
                pl.BlockSpec((step, ranks), lambda i, index: (jnp.maximum(i - half, 0), 0)),
            ],
            scratch_shapes=[pltpu.VMEM((features, ranks), BF16)],
        ),
        out_shape=[shape, shape],
        compiler_params=pltpu.CompilerParams(vmem_limit_bytes=VMEM_LIMIT),
        cost_estimate=pl.CostEstimate(
            flops=2 * tokens * features * ranks, bytes_accessed=2 * tokens * features, transcendentals=0
        ),
    )(index, *blocks, activations)


def sum_columns(ring, send, keep):
    mp, half = ring.mp, ring.mp // 2
    step = keep.shape[0] // half

    def move(value, core_step, other_step):
        pairs = []
        for d in range(ring.dp):
            for m in range(mp):
                other, core = divmod(m, 2)
                to = ((other + other_step) % half) * 2 + (core + core_step) % 2
                pairs.append((d * mp + m, d * mp + to))
        return lax.ppermute(value, AXES, pairs)

    from_core = move(send, 1, 0)
    total = None
    own = keep[(half - 1) * step :] + from_core[(half - 1) * step :]
    for j in range(half - 1):
        rows = slice(j * step, (j + 1) * step)
        own = own + move(keep[rows] + from_core[rows], 0, j + 1)
    own = own.astype(BF16)
    same = [own] + [move(own, 0, j) for j in range(1, half)]
    crossed = [move(value, 1, 0) for value in same]
    return same + crossed


def grad_rows(ring, index, pieces, out_grads, swapped):
    tokens, columns = out_grads.shape
    ranks = pieces[0].shape[1]
    mp, n = ring.mp, ring.n
    half, step = mp // 2, tokens // mp
    rows = ranks // ring.dp
    tile = tile_of(columns)

    def kernel(index_ref, *refs):
        pieces, (grads_ref, *outs), (held, turned, picked) = refs[:mp], refs[mp:-3], refs[-3:]
        line, pair, core, other = (index_ref[j] for j in range(4))

        @pl.when(pl.program_id(0) == 0)
        def _():
            for side in range(2):
                for j in range(half):
                    place = (core if side == 0 else 1 - core) * half + lax.rem(other - j + half, half)
                    held[pl.ds(pl.multiple_of(place * step, step), step), :] = pieces[side * half + j][...]
            turned[...] = held[...].T
            for r in range(n):
                start = (slot(line, r, n) * 2 + (1 - pair if swapped else pair)) * rows
                picked[r * rows : (r + 1) * rows, :] = turned[pl.ds(pl.multiple_of(start, rows), rows), :]

        value = jnp.dot(picked[...], grads_ref[...], preferred_element_type=F32).astype(BF16)
        for r in range(n):
            outs[r][...] = value[r * rows : (r + 1) * rows, :]

    return pl.pallas_call(
        kernel,
        grid_spec=pltpu.PrefetchScalarGridSpec(
            num_scalar_prefetch=1,
            grid=(columns // tile,),
            in_specs=[pl.BlockSpec((step, ranks), lambda i, index: (0, 0))] * mp
            + [pl.BlockSpec((tokens, tile), lambda i, index: (0, i))],
            out_specs=[pl.BlockSpec((rows, tile), lambda i, index: (0, i))] * n,
            scratch_shapes=[
                pltpu.VMEM((tokens, ranks), BF16),
                pltpu.VMEM((ranks, tokens), BF16),
                pltpu.VMEM((n * rows, tokens), BF16),
            ],
        ),
        out_shape=[jax.ShapeDtypeStruct((rows, columns), BF16)] * n,
        compiler_params=pltpu.CompilerParams(vmem_limit_bytes=VMEM_LIMIT),
        cost_estimate=pl.CostEstimate(
            flops=tokens * columns * ranks, bytes_accessed=2 * tokens * columns, transcendentals=0
        ),
    )(index, *pieces, out_grads)


def make_update(ring, index, blocks, basis):
    rows, ranks = basis.shape
    columns = blocks[0].shape[1]
    tile = tile_of(columns)

    def kernel(index_ref, *refs):
        pieces, (basis_ref, out_ref, held) = refs[: len(blocks)], refs[len(blocks) :]
        ring.assemble(index_ref, pieces, held)
        out_ref[...] = jnp.dot(basis_ref[...], held[...], preferred_element_type=F32).astype(BF16)

    return pl.pallas_call(
        kernel,
        grid_spec=pltpu.PrefetchScalarGridSpec(
            num_scalar_prefetch=1,
            grid=(columns // tile,),
            in_specs=[pl.BlockSpec((b.shape[0], tile), lambda i, index: (0, i)) for b in blocks]
            + [pl.BlockSpec((rows, ranks), lambda i, index: (0, 0))],
            out_specs=pl.BlockSpec((rows, tile), lambda i, index: (0, i)),
            scratch_shapes=[pltpu.VMEM((ranks, tile), BF16)],
        ),
        out_shape=jax.ShapeDtypeStruct((rows, columns), BF16),
        compiler_params=pltpu.CompilerParams(vmem_limit_bytes=VMEM_LIMIT),
        cost_estimate=pl.CostEstimate(
            flops=2 * rows * columns * ranks, bytes_accessed=2 * rows * columns, transcendentals=0
        ),
    )(index, *blocks, basis)


def solution(mesh):
    ring = Ring(mesh.shape["dp"], mesh.shape["mp"])

    def local(activations, out_grads, basis, first_moment, second_moment):
        d, m = lax.axis_index("dp"), lax.axis_index("mp")
        index = jnp.stack([d // 2, d % 2, m % 2, m // 2]).astype(jnp.int32)
        piece = scatter_basis(basis, activations.shape[1], ring.dp, ring.mp)
        send, keep = project(ring, index, ring.gather(piece), activations)
        projected = sum_columns(ring, send, keep)
        to_swap = grad_rows(ring, index, projected, out_grads, True)
        to_keep = grad_rows(ring, index, projected, out_grads, False)
        gradient = ring.scatter_sum(to_swap, to_keep)
        moment_one = BETA_ONE * first_moment + (1.0 - BETA_ONE) * gradient
        moment_two = BETA_TWO * second_moment + (1.0 - BETA_TWO) * gradient * gradient
        unbiased_one = moment_one / (1.0 - BETA_ONE**STEP)
        unbiased_two = moment_two / (1.0 - BETA_TWO**STEP)
        direction = (unbiased_one / (jnp.sqrt(unbiased_two) + ADAM_EPS)).astype(BF16)
        update = make_update(ring, index, ring.gather(direction), basis)
        return (update, moment_one, moment_two)

    return jax.shard_map(
        local,
        mesh=mesh,
        in_specs=(P("dp", "mp"), P("dp", "mp"), P("dp", None), P("dp", "mp"), P("dp", "mp")),
        out_specs=(P("dp", "mp"), P("dp", "mp"), P("dp", "mp")),
        check_vma=False,
    )
```

```python
import functools

import jax
import jax.numpy as jnp
from jax import lax
from jax.experimental import pallas as pl
from jax.experimental.pallas import tpu as pltpu
from jax.sharding import PartitionSpec as P

STEP = 10

BETA_ONE = 0.9
BETA_TWO = 0.999
ADAM_EPS = 1e-08

BF16 = jnp.bfloat16
F32 = jnp.float32
VMEM_LIMIT = 48 * 1024 * 1024
AXES = ("dp", "mp")
PARTS = 2
HALVES = 2
ANYWHERE = pl.BlockSpec(memory_space=pltpu.MemorySpace.HBM)


def tile_of(columns):
    for tile in (896, 512, 256, 128):
        if columns % tile == 0:
            return tile
    return columns


class Cube:
    def __init__(self, dp, mp):
        self.dp, self.mp = dp, mp
        self.order = [1 << j for j in range(dp.bit_length() - 1)]

    def swap(self, value, bit):
        pairs = [(d * self.mp + m, (d ^ bit) * self.mp + m) for d in range(self.dp) for m in range(self.mp)]
        return lax.ppermute(value, AXES, pairs)

    def sum_order(self):
        k = len(self.order)
        return [
            sum(bit for j, bit in enumerate(self.order) if not (p >> (k - 1 - j)) & 1) for p in range(self.dp)
        ]

    def gather_order(self):
        later = self.order[:1:-1]
        base = [sum(bit for j, bit in enumerate(later) if (i >> j) & 1) for i in range(1 << len(later))]
        first, second = self.order[:2]
        return [[r | extra for r in base] for extra in (0, second, first, first | second)]

    def sum_up(self, quarters):
        sent_first, sent_last, next_out, kept = quarters
        first, second = self.order[:2]
        got_first, got_last = self.swap(sent_first, first), self.swap(sent_last, first)
        out = (next_out.astype(F32) + got_first.astype(F32)).astype(BF16)
        terms = [(kept, 0), (got_last, 0), (self.swap(out, second), 0)]
        rows = kept.shape[0]
        for bit in self.order[2:]:
            rows //= 2
            out = sum(t[at : at + rows].astype(F32) for t, at in terms).astype(BF16)
            terms = [(t, at + rows) for t, at in terms] + [(self.swap(out, bit), 0)]
        return terms

    def gather(self, own):
        first, second = self.order[:2]
        for bit in self.order[:1:-1]:
            own = jnp.concatenate([own, self.swap(own, bit)])
        across = self.swap(own, second)
        return [own, across, self.swap(own, first), self.swap(across, first)]


def split_ranks(basis, dp, part, parts, wait_for):
    if parts == 1:
        return basis
    rows, ranks = basis.shape
    share = ranks // dp
    sub = share // parts

    def kernel(basis_ref, *refs):
        source = lax.broadcasted_iota(jnp.int32, (ranks, ranks // parts), 0)
        target = lax.broadcasted_iota(jnp.int32, (ranks, ranks // parts), 1)
        wanted = (target // sub) * share + part * sub + target % sub
        pick = jnp.where(source == wanted, 1.0, 0.0).astype(BF16)
        refs[-1][...] = jnp.dot(basis_ref[...], pick, preferred_element_type=F32).astype(BF16)

    return pl.pallas_call(
        kernel,
        in_specs=[pl.BlockSpec(basis.shape)] + [ANYWHERE] * len(wait_for),
        out_shape=jax.ShapeDtypeStruct((rows, ranks // parts), BF16),
        compiler_params=pltpu.CompilerParams(vmem_limit_bytes=VMEM_LIMIT),
    )(basis, *wait_for)


def fetch_basis(cube, basis):
    dp, mp = cube.dp, cube.mp
    shards = max(dp // mp // 2, 1)
    here = []
    for j in range(shards):
        pairs = []
        for line in range(dp // 2):
            q = line // shards
            for pair in range(2):
                for m in range(mp):
                    holder = ((q + m) % (mp // 2)) * 2 + q // (mp // 2)
                    source = (m * shards + (line + j) % shards) * 2 + pair
                    pairs.append((source * mp + holder, (line * 2 + pair) * mp + m))
        here.append(lax.ppermute(basis, AXES, pairs))
    return here


def project(cube, index, blocks, activations, wait_for):
    tokens, features = activations.shape
    rows, ranks = blocks[0].shape
    shards = len(blocks) // 2
    half = cube.mp // 2
    step = tokens // (2 * half)

    def block_of(i, index):
        return jnp.where(i < half, 1 - index[1], index[1]) * half + lax.rem(i, half)

    def kernel(index_ref, *refs):
        pieces, act_ref, (send_ref, keep_ref, held) = refs[: 2 * shards], refs[2 * shards], refs[-3:]
        i = pl.program_id(0)

        @pl.when(i == 0)
        def _():
            line, pair = index_ref[0] // 2, lax.rem(index_ref[0], 2)
            for j in range(2 * shards):
                side = pair if j < shards else 1 - pair
                start = (lax.rem(line + j, shards) * 2 + side) * rows
                held[pl.ds(pl.multiple_of(start, rows), rows), :] = pieces[j][...]

        value = jnp.dot(act_ref[...], held[...], preferred_element_type=F32)

        @pl.when(i < half)
        def _():
            send_ref[...] = value

        @pl.when(i >= half)
        def _():
            keep_ref[...] = value

    shape = jax.ShapeDtypeStruct((tokens // 2, ranks), F32)
    return pl.pallas_call(
        kernel,
        grid_spec=pltpu.PrefetchScalarGridSpec(
            num_scalar_prefetch=1,
            grid=(2 * half,),
            in_specs=[pl.BlockSpec(b.shape, lambda i, index: (0, 0)) for b in blocks]
            + [pl.BlockSpec((step, features), lambda i, index: (block_of(i, index), 0))]
            + [ANYWHERE] * len(wait_for),
            out_specs=[
                pl.BlockSpec((step, ranks), lambda i, index: (jnp.minimum(i, half - 1), 0)),
                pl.BlockSpec((step, ranks), lambda i, index: (jnp.maximum(i - half, 0), 0)),
            ],
            scratch_shapes=[pltpu.VMEM((features, ranks), BF16)],
        ),
        out_shape=[shape, shape],
        compiler_params=pltpu.CompilerParams(vmem_limit_bytes=VMEM_LIMIT),
        cost_estimate=pl.CostEstimate(
            flops=2 * tokens * features * ranks, bytes_accessed=2 * tokens * features, transcendentals=0
        ),
    )(index, *blocks, activations, *wait_for)


def sum_columns(cube, send, keep):
    mp, half = cube.mp, cube.mp // 2

    def move(value, core_step, other_step):
        pairs = []
        for d in range(cube.dp):
            for m in range(mp):
                other, core = divmod(m, 2)
                to = ((other + other_step) % half) * 2 + (core + core_step) % 2
                pairs.append((d * mp + m, d * mp + to))
        return lax.ppermute(value, AXES, pairs)

    chip = keep + move(send, 1, 0)
    total = chip
    for j in range(1, half):
        total = total + move(chip, 0, j)
    own = total.astype(BF16)
    return own, move(own, 1, 0)


def grad_rows(cube, index, pieces, out_grads, first_column, columns, wait_for):
    tokens = out_grads.shape[0]
    ranks = pieces[0].shape[1]
    rows = ranks // cube.dp
    quarter = ranks // 4
    tile = tile_of(columns)
    order = cube.sum_order()

    def kernel(index_ref, own_ref, other_ref, grads_ref, *refs):
        outs, (held, turned, picked) = refs[-7:-3], refs[-3:]
        here, core = index_ref[0], index_ref[1]

        @pl.when(pl.program_id(0) == 0)
        def _():
            half = tokens // 2
            held[pl.ds(pl.multiple_of(core * half, half), half), :] = own_ref[...]
            held[pl.ds(pl.multiple_of((1 - core) * half, half), half), :] = other_ref[...]
            turned[...] = held[...].T
            for p, relative in enumerate(order):
                start = pl.multiple_of((here ^ relative) * rows, rows)
                picked[p * rows : (p + 1) * rows, :] = turned[pl.ds(start, rows), :]

        value = jnp.dot(picked[...], grads_ref[...], preferred_element_type=F32).astype(BF16)
        for j in range(4):
            outs[j][...] = value[j * quarter : (j + 1) * quarter, :]

    return pl.pallas_call(
        kernel,
        grid_spec=pltpu.PrefetchScalarGridSpec(
            num_scalar_prefetch=1,
            grid=(columns // tile,),
            in_specs=[pl.BlockSpec((tokens // 2, ranks), lambda i, index: (0, 0))] * 2
            + [pl.BlockSpec((tokens, tile), lambda i, index: (0, first_column // tile + i))]
            + [ANYWHERE] * len(wait_for),
            out_specs=[pl.BlockSpec((quarter, tile), lambda i, index: (0, i))] * 4,
            scratch_shapes=[
                pltpu.VMEM((tokens, ranks), BF16),
                pltpu.VMEM((ranks, tokens), BF16),
                pltpu.VMEM((ranks, tokens), BF16),
            ],
        ),
        out_shape=[jax.ShapeDtypeStruct((quarter, columns), BF16)] * 4,
        compiler_params=pltpu.CompilerParams(vmem_limit_bytes=VMEM_LIMIT),
        cost_estimate=pl.CostEstimate(
            flops=2 * tokens * columns * ranks, bytes_accessed=2 * tokens * columns, transcendentals=0
        ),
    )(index, *pieces, out_grads, *wait_for)


def adam(cube, terms, first_moment, second_moment, part, first_column, before, wait_for):
    columns = terms[0][0].shape[1]
    share, width = first_moment.shape
    rows = terms[-1][0].shape[0]
    count = len(terms)

    def kernel(*refs):
        gradient = refs[0][...].astype(F32)
        for ref in refs[1:count]:
            gradient = gradient + ref[...].astype(F32)
        first_ref, second_ref = refs[count : count + 2]
        direction_ref, one_ref, two_ref = refs[-3:]
        moment_one = BETA_ONE * first_ref[...] + (1.0 - BETA_ONE) * gradient
        moment_two = BETA_TWO * second_ref[...] + (1.0 - BETA_TWO) * gradient * gradient
        unbiased_one = moment_one / (1.0 - BETA_ONE**STEP)
        unbiased_two = moment_two / (1.0 - BETA_TWO**STEP)
        direction_ref[...] = (unbiased_one / (jnp.sqrt(unbiased_two) + ADAM_EPS)).astype(BF16)
        one_ref[...] = moment_one
        two_ref[...] = moment_two

    term_specs = [pl.BlockSpec((rows, columns), lambda i, at=at // rows: (at, 0)) for _, at in terms]
    moment_spec = pl.BlockSpec((rows, columns), lambda i: (part, first_column // columns))
    moment = jax.ShapeDtypeStruct((share, width), F32)
    return pl.pallas_call(
        kernel,
        grid=(1,),
        in_specs=term_specs + [moment_spec] * 2 + [ANYWHERE] * len(before + wait_for),
        out_specs=[pl.BlockSpec((rows, columns), lambda i: (0, 0)), moment_spec, moment_spec],
        out_shape=[jax.ShapeDtypeStruct((rows, columns), BF16), moment, moment],
        input_output_aliases={count + 2: 1, count + 3: 2} if before else {},
        compiler_params=pltpu.CompilerParams(vmem_limit_bytes=VMEM_LIMIT),
        cost_estimate=pl.CostEstimate(
            flops=16 * rows * columns, bytes_accessed=26 * rows * columns, transcendentals=rows * columns
        ),
    )(*(t for t, _ in terms), first_moment, second_moment, *before, *wait_for)


def make_update(cube, index, groups, basis, first_column, width, before):
    rows, ranks = basis.shape
    parts = len(groups)
    columns = groups[0][0].shape[1]
    share = ranks // cube.dp
    sub = share // parts
    tile = tile_of(columns)
    blocks = [b for group in groups for b in group]
    order = cube.gather_order()

    def kernel(index_ref, *refs):
        pieces, basis_ref, (out_ref, held) = refs[: len(blocks)], refs[len(blocks)], refs[-2:]
        here = index_ref[0]
        for part in range(parts):
            for j, relatives in enumerate(order):
                for i, relative in enumerate(relatives):
                    start = pl.multiple_of((here ^ relative) * share + part * sub, sub)
                    held[pl.ds(start, sub), :] = pieces[part * 4 + j][i * sub : (i + 1) * sub, :]
        out_ref[...] = jnp.dot(basis_ref[...], held[...], preferred_element_type=F32).astype(BF16)

    return pl.pallas_call(
        kernel,
        grid_spec=pltpu.PrefetchScalarGridSpec(
            num_scalar_prefetch=1,
            grid=(columns // tile,),
            in_specs=[pl.BlockSpec((b.shape[0], tile), lambda i, index: (0, i)) for b in blocks]
            + [pl.BlockSpec((rows, ranks), lambda i, index: (0, 0))]
            + [ANYWHERE] * len(before),
            out_specs=pl.BlockSpec((rows, tile), lambda i, index: (0, first_column // tile + i)),
            scratch_shapes=[pltpu.VMEM((ranks, tile), BF16)],
        ),
        out_shape=jax.ShapeDtypeStruct((rows, width), BF16),
        input_output_aliases={len(blocks) + 2: 0} if before else {},
        compiler_params=pltpu.CompilerParams(vmem_limit_bytes=VMEM_LIMIT),
        cost_estimate=pl.CostEstimate(
            flops=2 * rows * columns * ranks, bytes_accessed=2 * rows * columns, transcendentals=0
        ),
    )(index, *blocks, basis, *before)


def solution(mesh):
    cube = Cube(mesh.shape["dp"], mesh.shape["mp"])

    def local(activations, out_grads, basis, first_moment, second_moment):
        d, m = lax.axis_index("dp"), lax.axis_index("mp")
        index = jnp.stack([d, m % 2]).astype(jnp.int32)
        share, width = first_moment.shape
        parts = PARTS if share % (16 * PARTS) == 0 else 1
        columns = width // HALVES
        here = []
        for h in range(parts):
            part = split_ranks(basis, cube.dp, h, parts, here[-1][:1] if here else [])
            here.append(fetch_basis(cube, part))
        partial = []
        for h in range(parts):
            blocks = here[h] + [cube.swap(value, 1) for value in here[h]]
            partial.append(project(cube, index, blocks, activations, []))
        groups, moments, update = [[None] * parts for _ in range(HALVES)], [], []
        terms = []
        for h in range(parts):
            projected = sum_columns(cube, *partial[h])
            for f in range(HALVES):
                wait_for = [partial[h + 1][0]] if h + 1 < parts else []
                quarters = grad_rows(cube, index, projected, out_grads, f * columns, columns, wait_for)
                terms.append((h, f, cube.sum_up(quarters)))
        for h, f, sums in terms:
            wait_for = groups[f][h - 1][1:] if h else []
            direction, *moments = adam(cube, sums, first_moment, second_moment, h, f * columns, moments, wait_for)
            groups[f][h] = cube.gather(direction)
        for f in range(HALVES):
            update = [make_update(cube, index, groups[f], basis, f * columns, width, update)]
        return (*update, *moments)

    return jax.shard_map(
        local,
        mesh=mesh,
        in_specs=(P("dp", "mp"), P("dp", "mp"), P("dp", None), P("dp", "mp"), P("dp", "mp")),
        out_specs=(P("dp", "mp"), P("dp", "mp"), P("dp", "mp")),
        check_vma=False,
    )
```

```python
import functools

import jax
import jax.numpy as jnp
from jax import lax
from jax.experimental import pallas as pl
from jax.experimental.pallas import tpu as pltpu
from jax.sharding import PartitionSpec as P

STEP = 10

BETA_ONE = 0.9
BETA_TWO = 0.999
ADAM_EPS = 1e-08

BF16 = jnp.bfloat16
F32 = jnp.float32
VMEM_LIMIT = 48 * 1024 * 1024
AXES = ("dp", "mp")
PARTS = 2
HALVES = 2
ANYWHERE = pl.BlockSpec(memory_space=pltpu.MemorySpace.HBM)


def tile_of(columns):
    for tile in (896, 512, 256, 128):
        if columns % tile == 0:
            return tile
    return columns


def add_after(one, other, wait_for):
    def kernel(one_ref, other_ref, *refs):
        refs[-1][...] = (one_ref[...].astype(F32) + other_ref[...].astype(F32)).astype(BF16)

    return pl.pallas_call(
        kernel,
        in_specs=[pl.BlockSpec(one.shape)] * 2 + [ANYWHERE] * len(wait_for),
        out_shape=jax.ShapeDtypeStruct(one.shape, BF16),
        compiler_params=pltpu.CompilerParams(vmem_limit_bytes=VMEM_LIMIT),
    )(one, other, *wait_for)


class Cube:
    def __init__(self, dp, mp):
        self.dp, self.mp = dp, mp
        bits = [1 << j for j in range(dp.bit_length() - 1)]
        self.pair_first = bits
        self.pair_last = bits[1:] + bits[:1]
        self.pair_mid = bits[1:2] + bits[:1] + bits[2:]

    def swap(self, value, bit):
        pairs = [(d * self.mp + m, (d ^ bit) * self.mp + m) for d in range(self.dp) for m in range(self.mp)]
        return lax.ppermute(value, AXES, pairs)

    def sum_order(self, order):
        k = len(order)
        return [sum(bit for j, bit in enumerate(order) if not (p >> (k - 1 - j)) & 1) for p in range(self.dp)]

    def gather_order(self, order):
        later = order[:1:-1]
        base = [sum(bit for j, bit in enumerate(later) if (i >> j) & 1) for i in range(1 << len(later))]
        first, second = order[:2]
        return [[r | extra for r in base] for extra in (0, second, first, first | second)]

    def sum_up(self, quarters, order, wait_for):
        sent_first, sent_last, next_out, kept = quarters
        first, second = order[:2]
        got_first, got_last = self.swap(sent_first, first), self.swap(sent_last, first)
        if wait_for:
            out = add_after(next_out, got_first, wait_for)
        else:
            out = (next_out.astype(F32) + got_first.astype(F32)).astype(BF16)
        terms = [(kept, 0), (got_last, 0), (self.swap(out, second), 0)]
        rows = kept.shape[0]
        for bit in order[2:]:
            rows //= 2
            out = sum(t[at : at + rows].astype(F32) for t, at in terms).astype(BF16)
            terms = [(t, at + rows) for t, at in terms] + [(self.swap(out, bit), 0)]
        return terms

    def gather(self, own, order):
        first, second = order[:2]
        for bit in order[:1:-1]:
            own = jnp.concatenate([own, self.swap(own, bit)])
        across = self.swap(own, second)
        return [own, across, self.swap(own, first), self.swap(across, first)]


def split_ranks(basis, dp, part, parts, wait_for):
    if parts == 1:
        return basis
    rows, ranks = basis.shape
    share = ranks // dp
    sub = share // parts

    def kernel(basis_ref, *refs):
        source = lax.broadcasted_iota(jnp.int32, (ranks, ranks // parts), 0)
        target = lax.broadcasted_iota(jnp.int32, (ranks, ranks // parts), 1)
        wanted = (target // sub) * share + part * sub + target % sub
        pick = jnp.where(source == wanted, 1.0, 0.0).astype(BF16)
        refs[-1][...] = jnp.dot(basis_ref[...], pick, preferred_element_type=F32).astype(BF16)

    return pl.pallas_call(
        kernel,
        in_specs=[pl.BlockSpec(basis.shape)] + [ANYWHERE] * len(wait_for),
        out_shape=jax.ShapeDtypeStruct((rows, ranks // parts), BF16),
        compiler_params=pltpu.CompilerParams(vmem_limit_bytes=VMEM_LIMIT),
    )(basis, *wait_for)


def fetch_basis(cube, basis):
    dp, mp = cube.dp, cube.mp
    shards = max(dp // mp // 2, 1)
    here = []
    for j in range(shards):
        pairs = []
        for line in range(dp // 2):
            q = line // shards
            for pair in range(2):
                for m in range(mp):
                    holder = ((q + m) % (mp // 2)) * 2 + q // (mp // 2)
                    source = (m * shards + (line + j) % shards) * 2 + pair
                    pairs.append((source * mp + holder, (line * 2 + pair) * mp + m))
        here.append(lax.ppermute(basis, AXES, pairs))
    return here


def project(cube, index, blocks, activations, wait_for):
    tokens, features = activations.shape
    rows, ranks = blocks[0].shape
    shards = len(blocks) // 2
    half = cube.mp // 2
    step = tokens // (2 * half)

    def block_of(i, index):
        return jnp.where(i < half, 1 - index[1], index[1]) * half + lax.rem(i, half)

    def kernel(index_ref, *refs):
        pieces, act_ref, (send_ref, keep_ref, held) = refs[: 2 * shards], refs[2 * shards], refs[-3:]
        i = pl.program_id(0)

        @pl.when(i == 0)
        def _():
            line, pair = index_ref[0] // 2, lax.rem(index_ref[0], 2)
            for j in range(2 * shards):
                side = pair if j < shards else 1 - pair
                start = (lax.rem(line + j, shards) * 2 + side) * rows
                held[pl.ds(pl.multiple_of(start, rows), rows), :] = pieces[j][...]

        value = jnp.dot(act_ref[...], held[...], preferred_element_type=F32)

        @pl.when(i < half)
        def _():
            send_ref[...] = value

        @pl.when(i >= half)
        def _():
            keep_ref[...] = value

    shape = jax.ShapeDtypeStruct((tokens // 2, ranks), F32)
    return pl.pallas_call(
        kernel,
        grid_spec=pltpu.PrefetchScalarGridSpec(
            num_scalar_prefetch=1,
            grid=(2 * half,),
            in_specs=[pl.BlockSpec(b.shape, lambda i, index: (0, 0)) for b in blocks]
            + [pl.BlockSpec((step, features), lambda i, index: (block_of(i, index), 0))]
            + [ANYWHERE] * len(wait_for),
            out_specs=[
                pl.BlockSpec((step, ranks), lambda i, index: (jnp.minimum(i, half - 1), 0)),
                pl.BlockSpec((step, ranks), lambda i, index: (jnp.maximum(i - half, 0), 0)),
            ],
            scratch_shapes=[pltpu.VMEM((features, ranks), BF16)],
        ),
        out_shape=[shape, shape],
        compiler_params=pltpu.CompilerParams(vmem_limit_bytes=VMEM_LIMIT),
        cost_estimate=pl.CostEstimate(
            flops=2 * tokens * features * ranks, bytes_accessed=2 * tokens * features, transcendentals=0
        ),
    )(index, *blocks, activations, *wait_for)


def sum_columns(cube, send, keep):
    mp, half = cube.mp, cube.mp // 2

    def move(value, core_step, other_step):
        pairs = []
        for d in range(cube.dp):
            for m in range(mp):
                other, core = divmod(m, 2)
                to = ((other + other_step) % half) * 2 + (core + core_step) % 2
                pairs.append((d * mp + m, d * mp + to))
        return lax.ppermute(value, AXES, pairs)

    chip = keep + move(send, 1, 0)
    total = chip
    for j in range(1, half):
        total = total + move(chip, 0, j)
    own = total.astype(BF16)
    return own, move(own, 1, 0)


def grad_rows(cube, index, pieces, out_grads, order, first_column, columns, wait_for):
    tokens = out_grads.shape[0]
    ranks = pieces[0].shape[1]
    rows = ranks // cube.dp
    quarter = ranks // 4
    tile = tile_of(columns)
    relatives = cube.sum_order(order)

    def kernel(index_ref, own_ref, other_ref, grads_ref, *refs):
        outs, (held, turned, picked) = refs[-7:-3], refs[-3:]
        here, core = index_ref[0], index_ref[1]

        @pl.when(pl.program_id(0) == 0)
        def _():
            half = tokens // 2
            held[pl.ds(pl.multiple_of(core * half, half), half), :] = own_ref[...]
            held[pl.ds(pl.multiple_of((1 - core) * half, half), half), :] = other_ref[...]
            turned[...] = held[...].T
            for p, relative in enumerate(relatives):
                start = pl.multiple_of((here ^ relative) * rows, rows)
                picked[p * rows : (p + 1) * rows, :] = turned[pl.ds(start, rows), :]

        value = jnp.dot(picked[...], grads_ref[...], preferred_element_type=F32).astype(BF16)
        for j in range(4):
            outs[j][...] = value[j * quarter : (j + 1) * quarter, :]

    return pl.pallas_call(
        kernel,
        grid_spec=pltpu.PrefetchScalarGridSpec(
            num_scalar_prefetch=1,
            grid=(columns // tile,),
            in_specs=[pl.BlockSpec((tokens // 2, ranks), lambda i, index: (0, 0))] * 2
            + [pl.BlockSpec((tokens, tile), lambda i, index: (0, first_column // tile + i))]
            + [ANYWHERE] * len(wait_for),
            out_specs=[pl.BlockSpec((quarter, tile), lambda i, index: (0, i))] * 4,
            scratch_shapes=[
                pltpu.VMEM((tokens, ranks), BF16),
                pltpu.VMEM((ranks, tokens), BF16),
                pltpu.VMEM((ranks, tokens), BF16),
            ],
        ),
        out_shape=[jax.ShapeDtypeStruct((quarter, columns), BF16)] * 4,
        compiler_params=pltpu.CompilerParams(vmem_limit_bytes=VMEM_LIMIT),
        cost_estimate=pl.CostEstimate(
            flops=2 * tokens * columns * ranks, bytes_accessed=2 * tokens * columns, transcendentals=0
        ),
    )(index, *pieces, out_grads, *wait_for)


def adam(cube, terms, first_moment, second_moment, part, first_column, before, wait_for):
    columns = terms[0][0].shape[1]
    share, width = first_moment.shape
    rows = terms[-1][0].shape[0]
    count = len(terms)

    def kernel(*refs):
        gradient = refs[0][...].astype(F32)
        for ref in refs[1:count]:
            gradient = gradient + ref[...].astype(F32)
        first_ref, second_ref = refs[count : count + 2]
        direction_ref, one_ref, two_ref = refs[-3:]
        moment_one = BETA_ONE * first_ref[...] + (1.0 - BETA_ONE) * gradient
        moment_two = BETA_TWO * second_ref[...] + (1.0 - BETA_TWO) * gradient * gradient
        unbiased_one = moment_one / (1.0 - BETA_ONE**STEP)
        unbiased_two = moment_two / (1.0 - BETA_TWO**STEP)
        direction_ref[...] = (unbiased_one / (jnp.sqrt(unbiased_two) + ADAM_EPS)).astype(BF16)
        one_ref[...] = moment_one
        two_ref[...] = moment_two

    term_specs = [pl.BlockSpec((rows, columns), lambda i, at=at // rows: (at, 0)) for _, at in terms]
    moment_spec = pl.BlockSpec((rows, columns), lambda i: (part, first_column // columns))
    moment = jax.ShapeDtypeStruct((share, width), F32)
    return pl.pallas_call(
        kernel,
        grid=(1,),
        in_specs=term_specs + [moment_spec] * 2 + [ANYWHERE] * len(before + wait_for),
        out_specs=[pl.BlockSpec((rows, columns), lambda i: (0, 0)), moment_spec, moment_spec],
        out_shape=[jax.ShapeDtypeStruct((rows, columns), BF16), moment, moment],
        input_output_aliases={count + 2: 1, count + 3: 2} if before else {},
        compiler_params=pltpu.CompilerParams(vmem_limit_bytes=VMEM_LIMIT),
        cost_estimate=pl.CostEstimate(
            flops=16 * rows * columns, bytes_accessed=26 * rows * columns, transcendentals=rows * columns
        ),
    )(*(t for t, _ in terms), first_moment, second_moment, *before, *wait_for)


def make_update(cube, index, groups, orders, basis, first_column, width, before):
    rows, ranks = basis.shape
    parts = len(groups)
    columns = groups[0][0].shape[1]
    share = ranks // cube.dp
    sub = share // parts
    tile = tile_of(columns)
    blocks = [b for group in groups for b in group]
    places = [cube.gather_order(order) for order in orders]

    def kernel(index_ref, *refs):
        pieces, basis_ref, (out_ref, held) = refs[: len(blocks)], refs[len(blocks)], refs[-2:]
        here = index_ref[0]
        for part in range(parts):
            for j, relatives in enumerate(places[part]):
                for i, relative in enumerate(relatives):
                    start = pl.multiple_of((here ^ relative) * share + part * sub, sub)
                    held[pl.ds(start, sub), :] = pieces[part * 4 + j][i * sub : (i + 1) * sub, :]
        out_ref[...] = jnp.dot(basis_ref[...], held[...], preferred_element_type=F32).astype(BF16)

    return pl.pallas_call(
        kernel,
        grid_spec=pltpu.PrefetchScalarGridSpec(
            num_scalar_prefetch=1,
            grid=(columns // tile,),
            in_specs=[pl.BlockSpec((b.shape[0], tile), lambda i, index: (0, i)) for b in blocks]
            + [pl.BlockSpec((rows, ranks), lambda i, index: (0, 0))]
            + [ANYWHERE] * len(before),
            out_specs=pl.BlockSpec((rows, tile), lambda i, index: (0, first_column // tile + i)),
            scratch_shapes=[pltpu.VMEM((ranks, tile), BF16)],
        ),
        out_shape=jax.ShapeDtypeStruct((rows, width), BF16),
        input_output_aliases={len(blocks) + 2: 0} if before else {},
        compiler_params=pltpu.CompilerParams(vmem_limit_bytes=VMEM_LIMIT),
        cost_estimate=pl.CostEstimate(
            flops=2 * rows * columns * ranks, bytes_accessed=2 * rows * columns, transcendentals=0
        ),
    )(index, *blocks, basis, *before)


def solution(mesh):
    cube = Cube(mesh.shape["dp"], mesh.shape["mp"])

    def local(activations, out_grads, basis, first_moment, second_moment):
        d, m = lax.axis_index("dp"), lax.axis_index("mp")
        index = jnp.stack([d, m % 2]).astype(jnp.int32)
        share, width = first_moment.shape
        parts = PARTS if share % (16 * PARTS) == 0 else 1
        columns = width // HALVES
        here = []
        for h in range(parts):
            part = split_ranks(basis, cube.dp, h, parts, here[-1][:1] if here else [])
            here.append(fetch_basis(cube, part))
        partial = []
        for h in range(parts):
            blocks = here[h] + [cube.swap(value, 1) for value in here[h]]
            partial.append(project(cube, index, blocks, activations, []))
        sums, quarters, groups, moments, update = {}, {}, [[None] * parts for _ in range(HALVES)], [], []
        projected = [sum_columns(cube, *value) for value in partial]
        sum_orders = [cube.pair_mid, cube.pair_first] if parts > 1 else [cube.pair_first]
        gather_orders = [cube.pair_first, cube.pair_first] if parts > 1 else [cube.pair_first]
        for h in range(parts):
            for f in range(HALVES):
                wait_for = []
                if h + 1 < parts:
                    wait_for = [partial[h + 1][0]]
                quarters[h, f] = grad_rows(
                    cube, index, projected[h], out_grads, sum_orders[h], f * columns, columns, wait_for
                )
        for h in range(parts):
            for f in range(HALVES):
                wait_for = [quarters[h + 1, g][0] for g in range(HALVES)] if h + 1 < parts and f else []
                sums[h, f] = cube.sum_up(quarters[h, f], sum_orders[h], wait_for)
        for h in range(parts):
            for f in range(HALVES):
                wait_for = groups[f][h - 1][1:] if h else []
                direction, *moments = adam(
                    cube, sums[h, f], first_moment, second_moment, h, f * columns, moments, wait_for
                )
                groups[f][h] = cube.gather(direction, gather_orders[h])
        for f in range(HALVES):
            update = [make_update(cube, index, groups[f], gather_orders, basis, f * columns, width, update)]
        return (*update, *moments)

    return jax.shard_map(
        local,
        mesh=mesh,
        in_specs=(P("dp", "mp"), P("dp", "mp"), P("dp", None), P("dp", "mp"), P("dp", "mp")),
        out_specs=(P("dp", "mp"), P("dp", "mp"), P("dp", "mp")),
        check_vma=False,
    )
```

```python
import itertools

import jax
import jax.numpy as jnp
from jax import lax
from jax.experimental import pallas as pl
from jax.experimental.pallas import tpu as pltpu
from jax.sharding import PartitionSpec as P

STEP = 10

BETA_ONE = 0.9
BETA_TWO = 0.999
ADAM_EPS = 1e-08

BF16 = jnp.bfloat16
F32 = jnp.float32
VMEM_LIMIT = 48 * 1024 * 1024
AXES = ("dp", "mp")
PARTS = 2
HALVES = 2
ANYWHERE = pl.BlockSpec(memory_space=pltpu.MemorySpace.HBM)


def tile_of(columns):
    for tile in (896, 512, 256, 128):
        if columns % tile == 0:
            return tile
    return columns


def add_after(one, other, wait_for):
    def kernel(one_ref, other_ref, *refs):
        refs[-1][...] = (one_ref[...].astype(F32) + other_ref[...].astype(F32)).astype(BF16)

    return pl.pallas_call(
        kernel,
        in_specs=[pl.BlockSpec(one.shape)] * 2 + [ANYWHERE] * len(wait_for),
        out_shape=jax.ShapeDtypeStruct(one.shape, BF16),
        compiler_params=pltpu.CompilerParams(vmem_limit_bytes=VMEM_LIMIT),
    )(one, other, *wait_for)


def join_after(one, other, wait_for):
    rows, columns = one.shape

    def kernel(one_ref, other_ref, *refs):
        refs[-1][:rows, :] = one_ref[...]
        refs[-1][rows:, :] = other_ref[...]

    return pl.pallas_call(
        kernel,
        in_specs=[pl.BlockSpec(one.shape)] * 2 + [ANYWHERE] * len(wait_for),
        out_shape=jax.ShapeDtypeStruct((2 * rows, columns), BF16),
        compiler_params=pltpu.CompilerParams(vmem_limit_bytes=VMEM_LIMIT),
    )(one, other, *wait_for)


class Cube:
    def __init__(self, dp, mp):
        self.dp, self.mp = dp, mp
        bits = [1 << j for j in range(dp.bit_length() - 1)]
        self.pair_first = bits
        self.pair_last = bits[1:] + bits[:1]
        self.pair_mid = bits[1:2] + bits[:1] + bits[2:]

    def swap(self, value, bit):
        pairs = [(d * self.mp + m, (d ^ bit) * self.mp + m) for d in range(self.dp) for m in range(self.mp)]
        return lax.ppermute(value, AXES, pairs)

    def sum_order(self, order):
        k = len(order)
        return [sum(bit for j, bit in enumerate(order) if not (p >> (k - 1 - j)) & 1) for p in range(self.dp)]

    def gather_order(self, order):
        later = order[:1:-1]
        base = [sum(bit for j, bit in enumerate(later) if (i >> j) & 1) for i in range(1 << len(later))]
        first, second = order[:2]
        return [[r | extra for r in base] for extra in (0, second, first, first | second)]

    def sum_up(self, quarters, order, wait_for):
        sent_first, sent_last, next_out, kept = quarters
        first, second = order[:2]
        got_first, got_last = self.swap(sent_first, first), self.swap(sent_last, first)
        if wait_for:
            out = add_after(next_out, got_first, wait_for)
        else:
            out = (next_out.astype(F32) + got_first.astype(F32)).astype(BF16)
        terms = [(kept, 0), (got_last, 0), (self.swap(out, second), 0)]
        rows = kept.shape[0]
        for bit in order[2:]:
            rows //= 2
            out = sum(t[at : at + rows].astype(F32) for t, at in terms).astype(BF16)
            terms = [(t, at + rows) for t, at in terms] + [(self.swap(out, bit), 0)]
        return terms

    def gather(self, own, order, wait_for):
        first, second = order[:2]
        for bit in order[:1:-1]:
            got = self.swap(own, bit)
            own = join_after(own, got, wait_for) if wait_for else jnp.concatenate([own, got])
        across = self.swap(own, second)
        return [own, across, self.swap(own, first), self.swap(across, first)]


def split_ranks(basis, dp, part, parts, wait_for):
    if parts == 1:
        return basis
    rows, ranks = basis.shape
    share = ranks // dp
    sub = share // parts

    def kernel(basis_ref, *refs):
        source = lax.broadcasted_iota(jnp.int32, (ranks, ranks // parts), 0)
        target = lax.broadcasted_iota(jnp.int32, (ranks, ranks // parts), 1)
        wanted = (target // sub) * share + part * sub + target % sub
        pick = jnp.where(source == wanted, 1.0, 0.0).astype(BF16)
        refs[-1][...] = jnp.dot(basis_ref[...], pick, preferred_element_type=F32).astype(BF16)

    return pl.pallas_call(
        kernel,
        in_specs=[pl.BlockSpec(basis.shape)] + [ANYWHERE] * len(wait_for),
        out_shape=jax.ShapeDtypeStruct((rows, ranks // parts), BF16),
        compiler_params=pltpu.CompilerParams(vmem_limit_bytes=VMEM_LIMIT),
    )(basis, *wait_for)


def fetch_basis(cube, basis):
    dp, mp = cube.dp, cube.mp
    shards = max(dp // mp // 2, 1)
    here = []
    for j in range(shards):
        pairs = []
        for line in range(dp // 2):
            q = line // shards
            for pair in range(2):
                for m in range(mp):
                    holder = ((q + m) % (mp // 2)) * 2 + q // (mp // 2)
                    source = (m * shards + (line + j) % shards) * 2 + pair
                    pairs.append((source * mp + holder, (line * 2 + pair) * mp + m))
        here.append(lax.ppermute(basis, AXES, pairs))
    return here


def project(cube, blocks, activations):
    tokens, features = activations.shape
    rows, ranks = blocks[0].shape
    shards = len(blocks) // 2
    d, core = lax.axis_index("dp"), lax.axis_index("mp") % 2
    if shards == 1:
        one, other = blocks
        held = jnp.where(d % 2 == 0, jnp.concatenate([one, other]), jnp.concatenate([other, one]))
    else:
        held = jnp.zeros((features, ranks), BF16)
        for j, block in enumerate(blocks):
            side = d % 2 if j < shards else 1 - d % 2
            start = ((d // 2 + j) % shards * 2 + side) * rows
            held = lax.dynamic_update_slice_in_dim(held, block, start, 0)

    def half(which):
        own = lax.dynamic_slice_in_dim(activations, which * (tokens // 2), tokens // 2, 0)
        return jnp.dot(own, held, preferred_element_type=F32)

    return half(1 - core), half(core)


def sum_columns(cube, send, keep):
    mp, half = cube.mp, cube.mp // 2

    def move(value, core_step, other_step):
        pairs = []
        for d in range(cube.dp):
            for m in range(mp):
                other, core = divmod(m, 2)
                to = ((other + other_step) % half) * 2 + (core + core_step) % 2
                pairs.append((d * mp + m, d * mp + to))
        return lax.ppermute(value, AXES, pairs)

    chip = keep + move(send, 1, 0)
    total = chip
    for j in range(1, half):
        total = total + move(chip, 0, j)
    own = total.astype(BF16)
    return own, move(own, 1, 0)


def grad_rows(cube, index, pieces, out_grads, order, first_column, columns, wait_for):
    tokens = out_grads.shape[0]
    ranks = pieces[0].shape[1]
    rows = ranks // cube.dp
    quarter = ranks // 4
    tile = tile_of(columns)
    relatives = cube.sum_order(order)

    def kernel(index_ref, own_ref, other_ref, grads_ref, *refs):
        outs, (held, turned, picked) = refs[-7:-3], refs[-3:]
        here, core = index_ref[0], index_ref[1]

        @pl.when(pl.program_id(0) == 0)
        def _():
            half = tokens // 2
            held[pl.ds(pl.multiple_of(core * half, half), half), :] = own_ref[...]
            held[pl.ds(pl.multiple_of((1 - core) * half, half), half), :] = other_ref[...]
            turned[...] = held[...].T
            for p, relative in enumerate(relatives):
                start = pl.multiple_of((here ^ relative) * rows, rows)
                picked[p * rows : (p + 1) * rows, :] = turned[pl.ds(start, rows), :]

        value = jnp.dot(picked[...], grads_ref[...], preferred_element_type=F32).astype(BF16)
        for j in range(4):
            outs[j][...] = value[j * quarter : (j + 1) * quarter, :]

    return pl.pallas_call(
        kernel,
        grid_spec=pltpu.PrefetchScalarGridSpec(
            num_scalar_prefetch=1,
            grid=(columns // tile,),
            in_specs=[pl.BlockSpec((tokens // 2, ranks), lambda i, index: (0, 0))] * 2
            + [pl.BlockSpec((tokens, tile), lambda i, index: (0, first_column // tile + i))]
            + [ANYWHERE] * len(wait_for),
            out_specs=[pl.BlockSpec((quarter, tile), lambda i, index: (0, i))] * 4,
            scratch_shapes=[
                pltpu.VMEM((tokens, ranks), BF16),
                pltpu.VMEM((ranks, tokens), BF16),
                pltpu.VMEM((ranks, tokens), BF16),
            ],
        ),
        out_shape=[jax.ShapeDtypeStruct((quarter, columns), BF16)] * 4,
        compiler_params=pltpu.CompilerParams(vmem_limit_bytes=VMEM_LIMIT),
        cost_estimate=pl.CostEstimate(
            flops=2 * tokens * columns * ranks, bytes_accessed=2 * tokens * columns, transcendentals=0
        ),
    )(index, *pieces, out_grads, *wait_for)


def adam(cube, terms, first_moment, second_moment, part, first_column, before, wait_for):
    columns = terms[0][0].shape[1]
    share, width = first_moment.shape
    rows = terms[-1][0].shape[0]
    count = len(terms)

    def kernel(*refs):
        gradient = refs[0][...].astype(F32)
        for ref in refs[1:count]:
            gradient = gradient + ref[...].astype(F32)
        first_ref, second_ref = refs[count : count + 2]
        direction_ref, one_ref, two_ref = refs[-3:]
        moment_one = BETA_ONE * first_ref[...] + (1.0 - BETA_ONE) * gradient
        moment_two = BETA_TWO * second_ref[...] + (1.0 - BETA_TWO) * gradient * gradient
        unbiased_one = moment_one / (1.0 - BETA_ONE**STEP)
        unbiased_two = moment_two / (1.0 - BETA_TWO**STEP)
        direction_ref[...] = (unbiased_one / (jnp.sqrt(unbiased_two) + ADAM_EPS)).astype(BF16)
        one_ref[...] = moment_one
        two_ref[...] = moment_two

    term_specs = [pl.BlockSpec((rows, columns), lambda i, at=at // rows: (at, 0)) for _, at in terms]
    moment_spec = pl.BlockSpec((rows, columns), lambda i: (part, first_column // columns))
    moment = jax.ShapeDtypeStruct((share, width), F32)
    return pl.pallas_call(
        kernel,
        grid=(1,),
        in_specs=term_specs + [moment_spec] * 2 + [ANYWHERE] * len(before + wait_for),
        out_specs=[pl.BlockSpec((rows, columns), lambda i: (0, 0)), moment_spec, moment_spec],
        out_shape=[jax.ShapeDtypeStruct((rows, columns), BF16), moment, moment],
        input_output_aliases={count + 2: 1, count + 3: 2} if before else {},
        compiler_params=pltpu.CompilerParams(vmem_limit_bytes=VMEM_LIMIT),
        cost_estimate=pl.CostEstimate(
            flops=16 * rows * columns, bytes_accessed=26 * rows * columns, transcendentals=rows * columns
        ),
    )(*(t for t, _ in terms), first_moment, second_moment, *before, *wait_for)


def make_update(cube, index, groups, orders, basis, first_column, width, before):
    rows, ranks = basis.shape
    parts = len(groups)
    columns = groups[0][0].shape[1]
    share = ranks // cube.dp
    sub = share // parts
    tile = tile_of(columns)
    blocks = [b for group in groups for b in group]
    places = [cube.gather_order(order) for order in orders]

    def kernel(index_ref, *refs):
        pieces, basis_ref, (out_ref, held) = refs[: len(blocks)], refs[len(blocks)], refs[-2:]
        here = index_ref[0]
        for part in range(parts):
            for j, relatives in enumerate(places[part]):
                for i, relative in enumerate(relatives):
                    start = pl.multiple_of((here ^ relative) * share + part * sub, sub)
                    held[pl.ds(start, sub), :] = pieces[part * 4 + j][i * sub : (i + 1) * sub, :]
        out_ref[...] = jnp.dot(basis_ref[...], held[...], preferred_element_type=F32).astype(BF16)

    return pl.pallas_call(
        kernel,
        grid_spec=pltpu.PrefetchScalarGridSpec(
            num_scalar_prefetch=1,
            grid=(columns // tile,),
            in_specs=[pl.BlockSpec((b.shape[0], tile), lambda i, index: (0, i)) for b in blocks]
            + [pl.BlockSpec((rows, ranks), lambda i, index: (0, 0))]
            + [ANYWHERE] * len(before),
            out_specs=pl.BlockSpec((rows, tile), lambda i, index: (0, first_column // tile + i)),
            scratch_shapes=[pltpu.VMEM((ranks, tile), BF16)],
        ),
        out_shape=jax.ShapeDtypeStruct((rows, width), BF16),
        input_output_aliases={len(blocks) + 2: 0} if before else {},
        compiler_params=pltpu.CompilerParams(vmem_limit_bytes=VMEM_LIMIT),
        cost_estimate=pl.CostEstimate(
            flops=2 * rows * columns * ranks, bytes_accessed=2 * rows * columns, transcendentals=0
        ),
    )(index, *blocks, basis, *before)


def solution(mesh):
    cube = Cube(mesh.shape["dp"], mesh.shape["mp"])

    def local(activations, out_grads, basis, first_moment, second_moment):
        d, m = lax.axis_index("dp"), lax.axis_index("mp")
        index = jnp.stack([d, m % 2]).astype(jnp.int32)
        share, width = first_moment.shape
        parts = PARTS if share % (16 * PARTS) == 0 else 1
        columns = width // HALVES
        here = []
        for h in range(parts):
            part = split_ranks(basis, cube.dp, h, parts, here[-1][:1] if here else [])
            here.append(fetch_basis(cube, part))
        partial = []
        for h in range(parts):
            blocks = here[h] + [cube.swap(value, 1) for value in here[h]]
            partial.append(project(cube, blocks, activations))
        sums, quarters, groups, moments, update = {}, {}, [[None] * parts for _ in range(HALVES)], [], []
        projected = [sum_columns(cube, *value) for value in partial]
        sum_order = {key: cube.pair_first for key in itertools.product(range(parts), range(HALVES))}
        gather_order = dict(sum_order)
        if parts > 1:
            sum_order[0, 0] = sum_order[0, 1] = cube.pair_mid
        for h in range(parts):
            for f in range(HALVES):
                wait_for = []
                if h + 1 < parts:
                    wait_for = [partial[h + 1][0]]
                quarters[h, f] = grad_rows(
                    cube, index, projected[h], out_grads, sum_order[h, f], f * columns, columns, wait_for
                )
        for h in range(parts):
            for f in range(HALVES):
                wait_for = [quarters[h + 1, g][0] for g in range(HALVES)] if h + 1 < parts and f else []
                sums[h, f] = cube.sum_up(quarters[h, f], sum_order[h, f], wait_for)
        for h in range(parts):
            directions = []
            for f in range(HALVES):
                wait_for = groups[f][h - 1][1:] if h else []
                direction, *moments = adam(
                    cube, sums[h, f], first_moment, second_moment, h, f * columns, moments, wait_for
                )
                directions.append(direction)
            for f in range(HALVES):
                wait_for = directions[f + 1 :] if h == parts - 1 else []
                groups[f][h] = cube.gather(directions[f], gather_order[h, f], wait_for)
        for f in range(HALVES):
            update = [make_update(cube, index, groups[f], [gather_order[h, f] for h in range(parts)], basis, f * columns, width, update)]
        return (*update, *moments)

    return jax.shard_map(
        local,
        mesh=mesh,
        in_specs=(P("dp", "mp"), P("dp", "mp"), P("dp", None), P("dp", "mp"), P("dp", "mp")),
        out_specs=(P("dp", "mp"), P("dp", "mp"), P("dp", "mp")),
        check_vma=False,
    )
```

```python
import itertools

import jax
import jax.numpy as jnp
from jax import lax
from jax.experimental import pallas as pl
from jax.experimental.pallas import tpu as pltpu
from jax.sharding import PartitionSpec as P

STEP = 10

BETA_ONE = 0.9
BETA_TWO = 0.999
ADAM_EPS = 1e-08

BF16 = jnp.bfloat16
F32 = jnp.float32
VMEM_LIMIT = 48 * 1024 * 1024
AXES = ("dp", "mp")
PARTS = 2
HALVES = 2
ANYWHERE = pl.BlockSpec(memory_space=pltpu.MemorySpace.HBM)


def tile_of(columns):
    for tile in (896, 512, 256, 128):
        if columns % tile == 0:
            return tile
    return columns


def add_after(one, other, wait_for):
    def kernel(one_ref, other_ref, *refs):
        refs[-1][...] = (one_ref[...].astype(F32) + other_ref[...].astype(F32)).astype(BF16)

    return pl.pallas_call(
        kernel,
        in_specs=[pl.BlockSpec(one.shape)] * 2 + [ANYWHERE] * len(wait_for),
        out_shape=jax.ShapeDtypeStruct(one.shape, BF16),
        compiler_params=pltpu.CompilerParams(vmem_limit_bytes=VMEM_LIMIT),
    )(one, other, *wait_for)


def join_after(one, other, wait_for):
    rows, columns = one.shape

    def kernel(one_ref, other_ref, *refs):
        refs[-1][:rows, :] = one_ref[...]
        refs[-1][rows:, :] = other_ref[...]

    return pl.pallas_call(
        kernel,
        in_specs=[pl.BlockSpec(one.shape)] * 2 + [ANYWHERE] * len(wait_for),
        out_shape=jax.ShapeDtypeStruct((2 * rows, columns), BF16),
        compiler_params=pltpu.CompilerParams(vmem_limit_bytes=VMEM_LIMIT),
    )(one, other, *wait_for)


class Cube:
    def __init__(self, dp, mp):
        self.dp, self.mp = dp, mp
        bits = [1 << j for j in range(dp.bit_length() - 1)]
        self.pair_first = bits
        self.pair_last = bits[1:] + bits[:1]
        self.pair_mid = bits[1:2] + bits[:1] + bits[2:]

    def swap(self, value, bit):
        pairs = [(d * self.mp + m, (d ^ bit) * self.mp + m) for d in range(self.dp) for m in range(self.mp)]
        return lax.ppermute(value, AXES, pairs)

    def sum_order(self, order):
        k = len(order)
        return [sum(bit for j, bit in enumerate(order) if not (p >> (k - 1 - j)) & 1) for p in range(self.dp)]

    def gather_order(self, order):
        later = order[:1:-1]
        base = [sum(bit for j, bit in enumerate(later) if (i >> j) & 1) for i in range(1 << len(later))]
        first, second = order[:2]
        return [[r | extra for r in base] for extra in (0, second, first, first | second)]

    def sum_up(self, quarters, order, wait_for):
        sent_first, sent_last, next_out, kept = quarters
        first, second = order[:2]
        got_first, got_last = self.swap(sent_first, first), self.swap(sent_last, first)
        if wait_for:
            out = add_after(next_out, got_first, wait_for)
        else:
            out = (next_out.astype(F32) + got_first.astype(F32)).astype(BF16)
        terms = [(kept, 0), (got_last, 0), (self.swap(out, second), 0)]
        rows = kept.shape[0]
        for bit in order[2:]:
            rows //= 2
            out = sum(t[at : at + rows].astype(F32) for t, at in terms).astype(BF16)
            terms = [(t, at + rows) for t, at in terms] + [(self.swap(out, bit), 0)]
        return terms

    def gather(self, own, order, wait_for):
        first, second = order[:2]
        for bit in order[:1:-1]:
            got = self.swap(own, bit)
            own = join_after(own, got, wait_for) if wait_for else jnp.concatenate([own, got])
        across = self.swap(own, second)
        return [own, across, self.swap(own, first), self.swap(across, first)]


def split_ranks(basis, dp, part, parts, wait_for):
    if parts == 1:
        return basis
    rows, ranks = basis.shape
    share = ranks // dp
    sub = share // parts

    def kernel(basis_ref, *refs):
        source = lax.broadcasted_iota(jnp.int32, (ranks, ranks // parts), 0)
        target = lax.broadcasted_iota(jnp.int32, (ranks, ranks // parts), 1)
        wanted = (target // sub) * share + part * sub + target % sub
        pick = jnp.where(source == wanted, 1.0, 0.0).astype(BF16)
        refs[-1][...] = jnp.dot(basis_ref[...], pick, preferred_element_type=F32).astype(BF16)

    return pl.pallas_call(
        kernel,
        in_specs=[pl.BlockSpec(basis.shape)] + [ANYWHERE] * len(wait_for),
        out_shape=jax.ShapeDtypeStruct((rows, ranks // parts), BF16),
        compiler_params=pltpu.CompilerParams(vmem_limit_bytes=VMEM_LIMIT),
    )(basis, *wait_for)


def fetch_basis(cube, basis):
    dp, mp = cube.dp, cube.mp
    shards = max(dp // mp // 2, 1)
    here = []
    for j in range(shards):
        pairs = []
        for line in range(dp // 2):
            q = line // shards
            for pair in range(2):
                for m in range(mp):
                    holder = ((q + m) % (mp // 2)) * 2 + q // (mp // 2)
                    source = (m * shards + (line + j) % shards) * 2 + pair
                    pairs.append((source * mp + holder, (line * 2 + pair) * mp + m))
        here.append(lax.ppermute(basis, AXES, pairs))
    return here


def project(cube, blocks, activations):
    tokens, features = activations.shape
    rows, ranks = blocks[0].shape
    shards = len(blocks) // 2
    d, core = lax.axis_index("dp"), lax.axis_index("mp") % 2
    if shards == 1:
        one, other = blocks
        held = jnp.where(d % 2 == 0, jnp.concatenate([one, other]), jnp.concatenate([other, one]))
    else:
        held = jnp.zeros((features, ranks), BF16)
        for j, block in enumerate(blocks):
            side = d % 2 if j < shards else 1 - d % 2
            start = ((d // 2 + j) % shards * 2 + side) * rows
            held = lax.dynamic_update_slice_in_dim(held, block, start, 0)

    def half(which):
        own = lax.dynamic_slice_in_dim(activations, which * (tokens // 2), tokens // 2, 0)
        return jnp.dot(own, held, preferred_element_type=F32)

    return half(1 - core), half(core)


def sum_columns(cube, send, keep):
    mp, half = cube.mp, cube.mp // 2

    def move(value, core_step, other_step):
        pairs = []
        for d in range(cube.dp):
            for m in range(mp):
                other, core = divmod(m, 2)
                to = ((other + other_step) % half) * 2 + (core + core_step) % 2
                pairs.append((d * mp + m, d * mp + to))
        return lax.ppermute(value, AXES, pairs)

    chip = keep + move(send, 1, 0)
    total = chip
    for j in range(1, half):
        total = total + move(chip, 0, j)
    own = total.astype(BF16)
    return own, move(own, 1, 0), chip


def grad_rows(cube, index, pieces, out_grads, order, first_column, columns, wait_for):
    tokens = out_grads.shape[0]
    ranks = pieces[0].shape[1]
    rows = ranks // cube.dp
    quarter = ranks // 4
    tile = tile_of(columns)
    relatives = cube.sum_order(order)

    def kernel(index_ref, own_ref, other_ref, grads_ref, *refs):
        outs, (held, turned, picked) = refs[-7:-3], refs[-3:]
        here, core = index_ref[0], index_ref[1]

        @pl.when(pl.program_id(0) == 0)
        def _():
            half = tokens // 2
            held[pl.ds(pl.multiple_of(core * half, half), half), :] = own_ref[...]
            held[pl.ds(pl.multiple_of((1 - core) * half, half), half), :] = other_ref[...]
            turned[...] = held[...].T
            for p, relative in enumerate(relatives):
                start = pl.multiple_of((here ^ relative) * rows, rows)
                picked[p * rows : (p + 1) * rows, :] = turned[pl.ds(start, rows), :]

        value = jnp.dot(picked[...], grads_ref[...], preferred_element_type=F32).astype(BF16)
        for j in range(4):
            outs[j][...] = value[j * quarter : (j + 1) * quarter, :]

    return pl.pallas_call(
        kernel,
        grid_spec=pltpu.PrefetchScalarGridSpec(
            num_scalar_prefetch=1,
            grid=(columns // tile,),
            in_specs=[pl.BlockSpec((tokens // 2, ranks), lambda i, index: (0, 0))] * 2
            + [pl.BlockSpec((tokens, tile), lambda i, index: (0, first_column // tile + i))]
            + [ANYWHERE] * len(wait_for),
            out_specs=[pl.BlockSpec((quarter, tile), lambda i, index: (0, i))] * 4,
            scratch_shapes=[
                pltpu.VMEM((tokens, ranks), BF16),
                pltpu.VMEM((ranks, tokens), BF16),
                pltpu.VMEM((ranks, tokens), BF16),
            ],
        ),
        out_shape=[jax.ShapeDtypeStruct((quarter, columns), BF16)] * 4,
        compiler_params=pltpu.CompilerParams(vmem_limit_bytes=VMEM_LIMIT),
        cost_estimate=pl.CostEstimate(
            flops=2 * tokens * columns * ranks, bytes_accessed=2 * tokens * columns, transcendentals=0
        ),
    )(index, *pieces, out_grads, *wait_for)


def adam(cube, terms, first_moment, second_moment, part, first_column, before, wait_for):
    columns = terms[0][0].shape[1]
    share, width = first_moment.shape
    rows = terms[-1][0].shape[0]
    count = len(terms)

    def kernel(*refs):
        gradient = refs[0][...].astype(F32)
        for ref in refs[1:count]:
            gradient = gradient + ref[...].astype(F32)
        first_ref, second_ref = refs[count : count + 2]
        direction_ref, one_ref, two_ref = refs[-3:]
        moment_one = BETA_ONE * first_ref[...] + (1.0 - BETA_ONE) * gradient
        moment_two = BETA_TWO * second_ref[...] + (1.0 - BETA_TWO) * gradient * gradient
        unbiased_one = moment_one / (1.0 - BETA_ONE**STEP)
        unbiased_two = moment_two / (1.0 - BETA_TWO**STEP)
        direction_ref[...] = (unbiased_one / (jnp.sqrt(unbiased_two) + ADAM_EPS)).astype(BF16)
        one_ref[...] = moment_one
        two_ref[...] = moment_two

    term_specs = [pl.BlockSpec((rows, columns), lambda i, at=at // rows: (at, 0)) for _, at in terms]
    moment_spec = pl.BlockSpec((rows, columns), lambda i: (part, first_column // columns))
    moment = jax.ShapeDtypeStruct((share, width), F32)
    return pl.pallas_call(
        kernel,
        grid=(1,),
        in_specs=term_specs + [moment_spec] * 2 + [ANYWHERE] * len(before + wait_for),
        out_specs=[pl.BlockSpec((rows, columns), lambda i: (0, 0)), moment_spec, moment_spec],
        out_shape=[jax.ShapeDtypeStruct((rows, columns), BF16), moment, moment],
        input_output_aliases={count + 2: 1, count + 3: 2} if before else {},
        compiler_params=pltpu.CompilerParams(vmem_limit_bytes=VMEM_LIMIT),
        cost_estimate=pl.CostEstimate(
            flops=16 * rows * columns, bytes_accessed=26 * rows * columns, transcendentals=rows * columns
        ),
    )(*(t for t, _ in terms), first_moment, second_moment, *before, *wait_for)


def make_update(cube, index, groups, orders, basis, first_column, width, before):
    rows, ranks = basis.shape
    parts = len(groups)
    columns = groups[0][0].shape[1]
    share = ranks // cube.dp
    sub = share // parts
    tile = tile_of(columns)
    blocks = [b for group in groups for b in group]
    places = [cube.gather_order(order) for order in orders]

    def kernel(index_ref, *refs):
        pieces, basis_ref, (out_ref, held) = refs[: len(blocks)], refs[len(blocks)], refs[-2:]
        here = index_ref[0]
        for part in range(parts):
            for j, relatives in enumerate(places[part]):
                for i, relative in enumerate(relatives):
                    start = pl.multiple_of((here ^ relative) * share + part * sub, sub)
                    held[pl.ds(start, sub), :] = pieces[part * 4 + j][i * sub : (i + 1) * sub, :]
        out_ref[...] = jnp.dot(basis_ref[...], held[...], preferred_element_type=F32).astype(BF16)

    return pl.pallas_call(
        kernel,
        grid_spec=pltpu.PrefetchScalarGridSpec(
            num_scalar_prefetch=1,
            grid=(columns // tile,),
            in_specs=[pl.BlockSpec((b.shape[0], tile), lambda i, index: (0, i)) for b in blocks]
            + [pl.BlockSpec((rows, ranks), lambda i, index: (0, 0))]
            + [ANYWHERE] * len(before),
            out_specs=pl.BlockSpec((rows, tile), lambda i, index: (0, first_column // tile + i)),
            scratch_shapes=[pltpu.VMEM((ranks, tile), BF16)],
        ),
        out_shape=jax.ShapeDtypeStruct((rows, width), BF16),
        input_output_aliases={len(blocks) + 2: 0} if before else {},
        compiler_params=pltpu.CompilerParams(vmem_limit_bytes=VMEM_LIMIT),
        cost_estimate=pl.CostEstimate(
            flops=2 * rows * columns * ranks, bytes_accessed=2 * rows * columns, transcendentals=0
        ),
    )(index, *blocks, basis, *before)


def solution(mesh):
    cube = Cube(mesh.shape["dp"], mesh.shape["mp"])

    def local(activations, out_grads, basis, first_moment, second_moment):
        d, m = lax.axis_index("dp"), lax.axis_index("mp")
        index = jnp.stack([d, m % 2]).astype(jnp.int32)
        share, width = first_moment.shape
        parts = PARTS if share % (16 * PARTS) == 0 else 1
        columns = width // HALVES
        here = []
        for h in range(parts):
            part = split_ranks(basis, cube.dp, h, parts, here[-1][:1] if here else [])
            here.append(fetch_basis(cube, part))
        partial = []
        for h in range(parts):
            blocks = here[h] + [cube.swap(value, 1) for value in here[h]]
            partial.append(project(cube, blocks, activations))
        sums, quarters, groups, moments, update = {}, {}, [[None] * parts for _ in range(HALVES)], [], []
        projected = [sum_columns(cube, *value) for value in partial]
        sum_order = {key: cube.pair_first for key in itertools.product(range(parts), range(HALVES))}
        gather_order = dict(sum_order)
        if parts > 1:
            sum_order[0, 0] = sum_order[0, 1] = cube.pair_mid
        for h in range(parts):
            for f in range(HALVES):
                wait_for = []
                if h + 1 < parts:
                    wait_for = [projected[h + 1][2]]
                quarters[h, f] = grad_rows(
                    cube, index, projected[h][:2], out_grads, sum_order[h, f], f * columns, columns, wait_for
                )
        for h in range(parts):
            for f in range(HALVES):
                wait_for = [quarters[h + 1, g][0] for g in range(HALVES)] if h + 1 < parts and f else []
                sums[h, f] = cube.sum_up(quarters[h, f], sum_order[h, f], wait_for)
        for h in range(parts):
            directions = []
            for f in range(HALVES):
                wait_for = groups[f][h - 1][1:] if h else []
                direction, *moments = adam(
                    cube, sums[h, f], first_moment, second_moment, h, f * columns, moments, wait_for
                )
                directions.append(direction)
            for f in range(HALVES):
                wait_for = directions[f + 1 :] if h == parts - 1 else []
                groups[f][h] = cube.gather(directions[f], gather_order[h, f], wait_for)
        for f in range(HALVES):
            update = [make_update(cube, index, groups[f], [gather_order[h, f] for h in range(parts)], basis, f * columns, width, update)]
        return (*update, *moments)

    return jax.shard_map(
        local,
        mesh=mesh,
        in_specs=(P("dp", "mp"), P("dp", "mp"), P("dp", None), P("dp", "mp"), P("dp", "mp")),
        out_specs=(P("dp", "mp"), P("dp", "mp"), P("dp", "mp")),
        check_vma=False,
    )
```
